32 devices in a mesh: group: 2 (over y), dp: 8 (over z, x), shard: 2 (over core).
Axes of the slice: x: 2, y: 2, z: 4, core: 2. Of those that a mesh axis runs over, the one named last changes fastest.
Arguments:
- inputs: bfloat16 [32, 16, 32, 256], P(('group', 'dp', 'shard')), parts along dimension 0, may hold values from -6 to 6
- cotangent: bfloat16 [32, 16, 32, 256], P(('group', 'dp', 'shard')), parts along dimension 0, may hold values from -6 to 6
- conv_first: bfloat16 [18, 256, 256], P('group', None, 'shard'), parts along dimension 0, may hold values from -0.125 to 0.125
- conv_second: bfloat16 [18, 256, 256], P('group', None, 'shard'), parts along dimension 0, may hold values from -0.125 to 0.125
Outputs:
- outputs: bfloat16 [32, 16, 32, 256], P(('group', 'dp', 'shard')), parts along dimension 0
- grad_first: bfloat16 [18, 256, 256], P('group', None, 'shard'), parts along dimension 0
- grad_second: bfloat16 [18, 256, 256], P('group', None, 'shard'), parts along dimension 0
The draws below stay inside these ranges and needn't reach their ends.
There are 2 independent parts, one for each index of `group`. The reference program is written for one: setup_inputs(seed, part) draws one part's arguments, and reference() takes and returns one part's arrays. A program takes and returns all parts, laid end to end along the dimension named above; each array names one. Nothing has to cross between parts.
All inputs are finite; a program needn't handle non-finite values.
Results may differ from the reference program's by a relative error of at most 0.012.
Values may be sent and summed in bfloat16 or wider, within the bound.
A program may use at most 64 MiB of HBM per device.

```python
import jax
import jax.numpy as jnp
from jax import lax

C = 256
HH = 16
WW = 32
SAMP_DEV = 1
SAMPLES = 16


def block_levels(stream_key, extent, split, low, largest):
    loudness, own = 1.0, jax.random.fold_in(stream_key, 6)
    for axis_at, shards_of in split:
        draws = jnp.exp(jax.random.uniform(jax.random.fold_in(own, axis_at), (shards_of,), jnp.float32, low / len(split), largest / len(split)))
        loudness = loudness * jnp.repeat(draws, extent[axis_at] // shards_of).reshape([-1 if axis == axis_at else 1 for axis in range(len(extent))])
    return loudness


def normal_values(rng, shape, spread, reach, shards=(), held_as=jnp.bfloat16):
    loudness = block_levels(rng, shape, shards, -0.22, 0.18) if shards else 1.0
    values = jax.random.normal(rng, shape, jnp.float32) * spread * loudness
    return jnp.minimum(jnp.maximum(values, -reach), reach).astype(held_as)


def setup_inputs(seed: int = 0, part: int = 0) -> dict:
    splits = jax.random.split(jax.random.key(seed), 5)
    part_splits = jax.random.split(jax.random.fold_in(splits[4], part), 5)
    inputs = normal_values(part_splits[0], (SAMPLES, HH, WW, C), 1.0, 6.0, ((0, 16),))
    cotangent = normal_values(part_splits[1], (SAMPLES, HH, WW, C), 1.0, 6.0, ((0, 16),))
    conv_first = normal_values(part_splits[2], (9, C, C), (9 * C) ** -0.5, 0.125, ((2, 2),))
    conv_second = normal_values(part_splits[3], (9, C, C), (9 * C) ** -0.5, 0.125, ((2, 2),))
    return dict(inputs=inputs, cotangent=cotangent, conv_first=conv_first, conv_second=conv_second)


def conv_taps(field, kernel):
    samples, rows, cols, chans = field.shape
    padded = jnp.pad(field, ((0, 0), (1, 1), (1, 1), (0, 0)))
    total = jnp.zeros((samples * rows * cols, kernel.shape[2]), jnp.float32)
    for tap in range(9):
        above = tap // 3
        left = tap % 3
        window = padded[:, above:above + rows, left:left + cols, :].reshape(-1, chans)
        total = total + jnp.dot(window, kernel[tap], preferred_element_type=jnp.float32)
    return total.reshape(samples, rows, cols, kernel.shape[2])


def flipped(kernel):
    return jnp.transpose(kernel[::-1], (0, 2, 1))


def weight_terms(field, grad):
    samples, rows, cols, chans = field.shape
    padded = jnp.pad(field, ((0, 0), (1, 1), (1, 1), (0, 0)))
    grad_flat = grad.reshape(-1, grad.shape[3])
    terms = []
    for tap in range(9):
        above = tap // 3
        left = tap % 3
        window = padded[:, above:above + rows, left:left + cols, :].reshape(-1, chans)
        terms.append(lax.dot_general(window, grad_flat, (((0,), (0,)), ((), ())), preferred_element_type=jnp.float32))
    return jnp.stack(terms, 0)


def rounded(value):
    return lax.optimization_barrier(value.astype(jnp.bfloat16)).astype(jnp.float32)


def reference(inputs, cotangent, conv_first, conv_second):
    pre = conv_taps(inputs, conv_first)
    hidden = jax.nn.silu(pre).astype(jnp.bfloat16)
    outputs = (inputs.astype(jnp.float32) + conv_taps(hidden, conv_second)).astype(jnp.bfloat16)
    back = conv_taps(cotangent, flipped(conv_second))
    sigma = jax.nn.sigmoid(pre)
    dpre = (back * sigma * (1.0 + pre * (1.0 - sigma))).astype(jnp.bfloat16)
    blocks = SAMPLES // SAMP_DEV
    shape = (blocks, SAMP_DEV, HH, WW, C)

    def step(carry, pieces):
        block_in, block_dpre, block_hidden, block_cot = pieces
        first = rounded(weight_terms(block_in, block_dpre))
        second = rounded(weight_terms(block_hidden, block_cot))
        return (carry[0] + first, carry[1] + second), None

    start = (jnp.zeros((9, C, C), jnp.float32), jnp.zeros((9, C, C), jnp.float32))
    sums, unused = lax.scan(step, start, (inputs.reshape(shape), dpre.reshape(shape), hidden.reshape(shape), cotangent.reshape(shape)))
    grad_first = (sums[0] / SAMPLES).astype(jnp.bfloat16)
    grad_second = (sums[1] / SAMPLES).astype(jnp.bfloat16)
    return (outputs, grad_first, grad_second)
```

```python
import functools

import jax
import jax.numpy as jnp
from jax import lax
from jax.experimental import pallas as pl
from jax.experimental.pallas import tpu as pltpu
from jax.sharding import PartitionSpec as P

MESH = pl.DeviceIdType.MESH
F32 = jnp.float32
BF16 = jnp.bfloat16
SUB = 1

PAIR, XRS, ZIN, ZMID, GZ, GX = range(6)


def remote(src, dst, ssem, rsem, dev):
    return pltpu.make_async_remote_copy(
        src_ref=src, dst_ref=dst, send_sem=ssem, recv_sem=rsem, device_id=dev, device_id_type=MESH
    )


def spread(dst, value, cols):
    cells, chans = value.shape
    j = lax.broadcasted_iota(jnp.int32, value.shape, 0) % cols
    zeros = jnp.zeros((cols, 3 * chans), BF16)
    dst[0:cols, :] = zeros
    dst[cells + cols : cells + 2 * cols, :] = zeros
    after = jnp.where(j == 0, 0.0, pltpu.roll(value, 1, 0))
    dst[cols : cells + cols, 0:chans] = after.astype(BF16)
    dst[cols : cells + cols, chans : 2 * chans] = value.astype(BF16)
    before = jnp.where(j == cols - 1, 0.0, pltpu.roll(value, cells - 1, 0))
    dst[cols : cells + cols, 2 * chans : 3 * chans] = before.astype(BF16)


def kernel(
    dims, x_hbm, g_hbm, w1_hbm, w2_hbm, out_hbm, g2_hbm, g1_hbm,
    xv, gv, wb1, wb2, sx, sh, sg, pre, gt, dt, ov,
    own, psend, precv, xsend, xrecv, zs, zin, zmid, gath,
    lsem, wsend, wrecv, ssem, rsem, osem,
):
    n, cols, scale = dims
    cells, chans = xv.shape
    half = chans // 2
    quarter = half // 2
    n_chunks, _, width = own.shape
    sub = 3 * chans // width
    line = n // 2

    dp = lax.axis_index("dp")
    me = lax.axis_index("shard")
    other = 1 - me
    xi = dp % 2
    z = dp // 2
    low = z < line // 2
    inward = jnp.where(low, z + 1, z - 1)
    outward = jnp.where(low, z - 1, z + 1)
    has_outer = jnp.logical_and(z > 0, z < line - 1)
    is_mid = jnp.logical_or(z == line // 2 - 1, z == line // 2)
    not_mid = jnp.logical_not(is_mid)
    to_pair = {"shard": other}
    to_x = {"dp": z * 2 + 1 - xi}
    to_in = {"dp": inward * 2 + xi}
    to_out = {"dp": outward * 2 + xi}

    locals_ = [
        pltpu.make_async_copy(x_hbm, xv, lsem.at[0]),
        pltpu.make_async_copy(w1_hbm, wb1.at[me], lsem.at[1]),
        pltpu.make_async_copy(g_hbm, gv, lsem.at[2]),
        pltpu.make_async_copy(w2_hbm, wb2.at[me], lsem.at[3]),
    ]
    for copy in locals_:
        copy.start()

    barrier = pltpu.get_barrier_semaphore()
    for dev in (to_pair, to_x, to_in):
        pl.semaphore_signal(barrier, inc=1, device_id=dev, device_id_type=MESH)

    @pl.when(has_outer)
    def _():
        pl.semaphore_signal(barrier, inc=1, device_id=to_out, device_id_type=MESH)

    pl.semaphore_wait(barrier, 3 + has_outer.astype(jnp.int32))

    wcopies = [
        remote(w1_hbm, wb1.at[me], wsend.at[0], wrecv.at[0], to_pair),
        remote(w2_hbm, wb2.at[me], wsend.at[1], wrecv.at[1], to_pair),
    ]
    for copy in wcopies:
        copy.start()

    my_rows = pl.ds(pl.multiple_of(xi * quarter, quarter), quarter)
    their_rows = pl.ds(pl.multiple_of((1 - xi) * quarter, quarter), quarter)

    def c_pair(q):
        return remote(psend.at[q], precv.at[q], ssem.at[PAIR, q], rsem.at[PAIR, q], to_pair)

    def c_xrs(q):
        return remote(xsend.at[q], xrecv.at[q], ssem.at[XRS, q], rsem.at[XRS, q], to_x)

    def c_zin(q):
        return remote(zs.at[q], zin.at[q], ssem.at[ZIN, q], rsem.at[ZIN, q], to_in)

    def c_zmid(q):
        return remote(zs.at[q], zmid.at[q], ssem.at[ZMID, q], rsem.at[ZMID, q], to_in)

    def c_gz(q):
        return remote(gath.at[q, my_rows], gath.at[q, my_rows], ssem.at[GZ, q], rsem.at[GZ, q], to_out)

    def c_gx(q):
        return remote(gath.at[q, my_rows], gath.at[q, my_rows], ssem.at[GX, q], rsem.at[GX, q], to_x)

    def c_out(q):
        per = n_chunks // 2
        dst = g2_hbm.at[q] if q < per else g1_hbm.at[q - per]
        return pltpu.make_async_copy(gath.at[q], dst, osem.at[q])

    def s1(q):
        c_pair(q).wait_recv()
        there = own[q, their_rows, :] + precv[q, their_rows, :].astype(F32)
        xsend[q] = there.astype(BF16)
        c_xrs(q).start()

    def s2(q):
        c_xrs(q).wait_recv()
        mine = own[q, my_rows, :] + precv[q, my_rows, :].astype(F32) + xrecv[q].astype(F32)

        @pl.when(has_outer)
        def _():
            own[q, my_rows, :] = mine

        @pl.when(jnp.logical_not(has_outer))
        def _():
            zs[q] = mine.astype(BF16)

    def s2b(q):
        @pl.when(jnp.logical_and(jnp.logical_not(has_outer), not_mid))
        def _():
            c_zin(q).start()

        @pl.when(jnp.logical_and(jnp.logical_not(has_outer), is_mid))
        def _():
            c_zmid(q).start()

    def s3(q):
        @pl.when(has_outer)
        def _():
            c_zin(q).wait_recv()
            zs[q] = (own[q, my_rows, :] + zin[q].astype(F32)).astype(BF16)

            @pl.when(is_mid)
            def _():
                c_zmid(q).start()

            @pl.when(not_mid)
            def _():
                c_zin(q).start()

    def s4(q):
        @pl.when(is_mid)
        def _():
            c_zmid(q).wait_recv()
            gath[q, my_rows, :] = ((zs[q].astype(F32) + zmid[q].astype(F32)) * scale).astype(BF16)
            c_gx(q).start()

            @pl.when(has_outer)
            def _():
                c_gz(q).start()

    def s5(q):
        @pl.when(not_mid)
        def _():
            c_gz(q).wait_recv()
            c_gx(q).start()

            @pl.when(has_outer)
            def _():
                c_gz(q).start()

    def s6(q):
        c_gx(q).wait_recv()
        c_out(q).start()

    stages = [s1, lambda q: (s2(q), s2b(q)), s3, s4, s5, s6]
    offsets = [0, 1, 2, 3, 4, 5]

    def tick(t):
        for stage, offset in reversed(list(zip(stages, offsets))):
            q = t - offset
            if 0 <= q < n_chunks:
                stage(q)

    def conv(src, kernel_halves, m0, m):
        left = jnp.concatenate([src[m0 + a * cols : m0 + a * cols + m, :] for a in range(3)], axis=1)
        right = jnp.concatenate([kernel_halves[0], kernel_halves[1]], axis=1)
        return jnp.dot(left, right, preferred_element_type=F32)

    def conv_back(src, kernel_halves, m0, m):
        left, right = [], []
        for tap in range(9):
            a, b = tap // 3, tap % 3
            rows = slice(m0 + (2 - a) * cols, m0 + (2 - a) * cols + m)
            left.append(src[rows, (2 - b) * chans : (3 - b) * chans])
            right.append(kernel_halves[0, tap * chans : (tap + 1) * chans, :])
            right.append(kernel_halves[1, tap * chans : (tap + 1) * chans, :])
        return lax.dot_general(
            jnp.concatenate(left, axis=1),
            jnp.concatenate(right, axis=1),
            (((1,), (1,)), ((), ())),
            preferred_element_type=F32,
        )

    def terms(grad_t, src, which, a):
        field = src[a * cols : a * cols + cells, :]
        there = jnp.dot(
            grad_t[pl.ds(pl.multiple_of(other * half, half), half), :], field, preferred_element_type=F32
        ).astype(BF16)
        for s in range(sub):
            q = (which * 3 + a) * sub + s
            psend[q] = there[:, s * width : (s + 1) * width]
            c_pair(q).start()
        here = jnp.dot(
            grad_t[pl.ds(pl.multiple_of(me * half, half), half), :], field, preferred_element_type=F32
        )
        for s in range(sub):
            q = (which * 3 + a) * sub + s
            own[q] = here[:, s * width : (s + 1) * width]

    tile = min(256, cells)
    locals_[0].wait()
    spread(sx, xv[...].astype(F32), cols)
    locals_[2].wait()
    gt[...] = gv[...].astype(F32).T.astype(BF16)
    spread(sg, gv[...].astype(F32), cols)
    locals_[1].wait()
    wcopies[0].wait_recv()
    for m0 in range(0, cells, tile):
        pre[m0 : m0 + tile, :] = conv(sx, wb1, m0, tile)
    v = pre[...]
    hidden = (v / (1.0 + jnp.exp(-v))).astype(BF16)
    spread(sh, hidden.astype(F32), cols)
    for a in range(3):
        terms(gt, sh, 0, a)
    locals_[3].wait()
    wcopies[1].wait_recv()
    s1(0)
    for m0 in range(0, cells, tile):
        back = conv_back(sg, wb2, m0, tile)
        v = pre[m0 : m0 + tile, :]
        sigma = 1.0 / (1.0 + jnp.exp(-v))
        dpre = back * sigma * (1.0 + v * (1.0 - sigma))
        dt[:, m0 : m0 + tile] = dpre.T.astype(BF16)
    per = n_chunks // 2
    done = 1
    for t in range(1, sub):
        tick(t)
        done = t + 1
    for a in range(3):
        terms(dt, sx, 1, a)
        for _ in range(sub):
            tick(done)
            done += 1
    m_out = min(128, cells)
    for m0 in range(0, cells, m_out):
        total = conv(sh, wb2, m0, m_out) + xv[m0 : m0 + m_out, :].astype(F32)
        ov[m0 : m0 + m_out, :] = total.astype(BF16)
        if done < n_chunks + offsets[-1]:
            tick(done)
            done += 1
    out_copy = pltpu.make_async_copy(ov, out_hbm, lsem.at[4])
    out_copy.start()
    while done < n_chunks + offsets[-1]:
        tick(done)
        done += 1

    for copy in wcopies:
        copy.wait_send()
    for q in range(n_chunks):
        c_pair(q).wait_send()
        c_xrs(q).wait_send()
        c_gx(q).wait_send()

        @pl.when(is_mid)
        def _():
            c_zmid(q).wait_send()

        @pl.when(not_mid)
        def _():
            c_zin(q).wait_send()

        @pl.when(has_outer)
        def _():
            c_gz(q).wait_send()

        c_out(q).wait()
    out_copy.wait()


def body(mesh, inputs, cotangent, conv_first, conv_second):
    _, rows, cols, chans = inputs.shape
    cells = rows * cols
    half = chans // 2
    n = mesh.shape["dp"]
    scale = 1.0 / (inputs.shape[0] * n * mesh.shape["shard"])
    width = 3 * chans // SUB
    n_chunks = 6 * SUB
    per = n_chunks // 2
    hbm = pl.BlockSpec(memory_space=pl.ANY)
    vm = pltpu.VMEM
    outputs, second, first = pl.pallas_call(
        functools.partial(kernel, (n, cols, scale)),
        out_shape=(
            jax.ShapeDtypeStruct((cells, chans), BF16),
            jax.ShapeDtypeStruct((per, half, width), BF16),
            jax.ShapeDtypeStruct((per, half, width), BF16),
        ),
        in_specs=[hbm] * 4,
        out_specs=(hbm, hbm, hbm),
        scratch_shapes=[
            vm((cells, chans), BF16),
            vm((cells, chans), BF16),
            vm((2, 9 * chans, half), BF16),
            vm((2, 9 * chans, half), BF16),
            vm((cells + 2 * cols, 3 * chans), BF16),
            vm((cells + 2 * cols, 3 * chans), BF16),
            vm((cells + 2 * cols, 3 * chans), BF16),
            vm((cells, chans), F32),
            vm((chans, cells), BF16),
            vm((chans, cells), BF16),
            vm((cells, chans), BF16),
            vm((n_chunks, half, width), F32),
            vm((n_chunks, half, width), BF16),
            vm((n_chunks, half, width), BF16),
            vm((n_chunks, half // 2, width), BF16),
            vm((n_chunks, half // 2, width), BF16),
            vm((n_chunks, half // 2, width), BF16),
            vm((n_chunks, half // 2, width), BF16),
            vm((n_chunks, half // 2, width), BF16),
            vm((n_chunks, half, width), BF16),
            pltpu.SemaphoreType.DMA((5,)),
            pltpu.SemaphoreType.DMA((2,)),
            pltpu.SemaphoreType.DMA((2,)),
            pltpu.SemaphoreType.DMA((6, n_chunks)),
            pltpu.SemaphoreType.DMA((6, n_chunks)),
            pltpu.SemaphoreType.DMA((n_chunks,)),
        ],
        compiler_params=pltpu.CompilerParams(
            collective_id=0, has_side_effects=True, vmem_limit_bytes=40 * 1024 * 1024
        ),
    )(
        inputs.reshape(cells, chans),
        cotangent.reshape(cells, chans),
        conv_first.reshape(9 * chans, half),
        conv_second.reshape(9 * chans, half),
    )

    def laid(grad):
        taps = grad.reshape(3, SUB, half, 3 // SUB, chans)
        return jnp.transpose(taps, (0, 1, 3, 4, 2)).reshape(9, chans, half)

    return outputs.reshape(inputs.shape), laid(first), laid(second)


def solution(mesh):
    placed = (
        P(("group", "dp", "shard"), None, None, None),
        P(("group", "dp", "shard"), None, None, None),
        P("group", None, "shard"),
        P("group", None, "shard"),
    )
    return jax.shard_map(
        functools.partial(body, mesh),
        mesh=mesh,
        in_specs=placed,
        out_specs=(
            P(("group", "dp", "shard"), None, None, None),
            P("group", None, "shard"),
            P("group", None, "shard"),
        ),
        check_vma=False,
    )
```

```python
import functools

import jax
import jax.numpy as jnp
from jax import lax
from jax.experimental import pallas as pl
from jax.experimental.pallas import tpu as pltpu
from jax.sharding import PartitionSpec as P

MESH = pl.DeviceIdType.MESH
F32 = jnp.float32
BF16 = jnp.bfloat16
SUB = 3
ROUTES = "A"
STEP = 5

PAIR, XRS, ZIN, ZMID, GZ, GX = range(6)


def remote(src, dst, ssem, rsem, dev):
    return pltpu.make_async_remote_copy(
        src_ref=src, dst_ref=dst, send_sem=ssem, recv_sem=rsem, device_id=dev, device_id_type=MESH
    )


def spread(dst, value, cols):
    cells, chans = value.shape
    j = lax.broadcasted_iota(jnp.int32, value.shape, 0) % cols
    zeros = jnp.zeros((cols, 3 * chans), BF16)
    dst[0:cols, :] = zeros
    dst[cells + cols : cells + 2 * cols, :] = zeros
    after = jnp.where(j == 0, 0.0, pltpu.roll(value, 1, 0))
    dst[cols : cells + cols, 0:chans] = after.astype(BF16)
    dst[cols : cells + cols, chans : 2 * chans] = value.astype(BF16)
    before = jnp.where(j == cols - 1, 0.0, pltpu.roll(value, cells - 1, 0))
    dst[cols : cells + cols, 2 * chans : 3 * chans] = before.astype(BF16)


def kernel(
    dims, x_hbm, g_hbm, w1_hbm, w2_hbm, out_hbm, g2_hbm, g1_hbm,
    xv, gv, wb1, wb2, sx, sh, sg, pre, gt, dt, ov,
    own, psend, precv, xsend, xrecv, zs, zin, zmid, gath, fs, fin, ob,
    lsem, wsend, wrecv, ssem, rsem, osem,
):
    n, cols, scale = dims
    cells, chans = xv.shape
    half = chans // 2
    quarter = half // 2
    n_chunks, _, width = own.shape
    sub = 3 * chans // width
    line = n // 2

    dp = lax.axis_index("dp")
    me = lax.axis_index("shard")
    other = 1 - me
    xi = dp % 2
    z = dp // 2
    low = z < line // 2
    inward = jnp.where(low, z + 1, z - 1)
    outward = jnp.where(low, z - 1, z + 1)
    has_outer = jnp.logical_and(z > 0, z < line - 1)
    is_mid = jnp.logical_or(z == line // 2 - 1, z == line // 2)
    not_mid = jnp.logical_not(is_mid)
    to_pair = {"shard": other}
    to_x = {"dp": z * 2 + 1 - xi}
    to_in = {"dp": inward * 2 + xi}
    to_out = {"dp": outward * 2 + xi}

    locals_ = [
        pltpu.make_async_copy(x_hbm, xv, lsem.at[0]),
        pltpu.make_async_copy(w1_hbm, wb1.at[me], lsem.at[1]),
        pltpu.make_async_copy(g_hbm, gv, lsem.at[2]),
        pltpu.make_async_copy(w2_hbm, wb2.at[me], lsem.at[3]),
    ]
    for copy in locals_:
        copy.start()

    barrier = pltpu.get_barrier_semaphore()
    for dev in (to_pair, to_x, to_in):
        pl.semaphore_signal(barrier, inc=1, device_id=dev, device_id_type=MESH)

    @pl.when(has_outer)
    def _():
        pl.semaphore_signal(barrier, inc=1, device_id=to_out, device_id_type=MESH)

    pl.semaphore_wait(barrier, 3 + has_outer.astype(jnp.int32))

    wcopies = [
        remote(w1_hbm, wb1.at[me], wsend.at[0], wrecv.at[0], to_pair),
        remote(w2_hbm, wb2.at[me], wsend.at[1], wrecv.at[1], to_pair),
    ]
    for copy in wcopies:
        copy.start()

    my_rows = pl.ds(pl.multiple_of(xi * quarter, quarter), quarter)
    their_rows = pl.ds(pl.multiple_of((1 - xi) * quarter, quarter), quarter)

    def c_pair(q):
        return remote(psend.at[q], precv.at[q], ssem.at[PAIR, q], rsem.at[PAIR, q], to_pair)

    def c_xrs(q):
        return remote(xsend.at[q], xrecv.at[q], ssem.at[XRS, q], rsem.at[XRS, q], to_x)

    def c_zin(q):
        return remote(zs.at[q], zin.at[q], ssem.at[ZIN, q], rsem.at[ZIN, q], to_in)

    def c_zmid(q):
        return remote(zs.at[q], zmid.at[q], ssem.at[ZMID, q], rsem.at[ZMID, q], to_in)

    def c_gz(q):
        return remote(gath.at[q, my_rows], gath.at[q, my_rows], ssem.at[GZ, q], rsem.at[GZ, q], to_out)

    def c_gx(q):
        return remote(gath.at[q, my_rows], gath.at[q, my_rows], ssem.at[GX, q], rsem.at[GX, q], to_x)

    def c_out(q):
        per = n_chunks // 2
        taps = width // chans
        dst = g2_hbm if q < per else g1_hbm
        at = q % per * taps
        return pltpu.make_async_copy(ob.at[q], dst.at[at : at + taps], osem.at[q])

    def finish(q):
        for k in range(width // chans):
            ob[q, k] = gath[q, :, k * chans : (k + 1) * chans].astype(F32).T.astype(BF16)
        c_out(q).start()

    def s1(q):
        c_pair(q).wait_recv()
        there = own[q, their_rows, :] + precv[q, their_rows, :].astype(F32)
        xsend[q] = there.astype(BF16)
        c_xrs(q).start()

    def s2(q):
        c_xrs(q).wait_recv()
        mine = own[q, my_rows, :] + precv[q, my_rows, :].astype(F32) + xrecv[q].astype(F32)

        @pl.when(has_outer)
        def _():
            own[q, my_rows, :] = mine

        @pl.when(jnp.logical_not(has_outer))
        def _():
            zs[q] = mine.astype(BF16)

    def s2b(q):
        @pl.when(jnp.logical_and(jnp.logical_not(has_outer), not_mid))
        def _():
            c_zin(q).start()

        @pl.when(jnp.logical_and(jnp.logical_not(has_outer), is_mid))
        def _():
            c_zmid(q).start()

    def s3(q):
        @pl.when(has_outer)
        def _():
            c_zin(q).wait_recv()
            zs[q] = (own[q, my_rows, :] + zin[q].astype(F32)).astype(BF16)

            @pl.when(is_mid)
            def _():
                c_zmid(q).start()

            @pl.when(not_mid)
            def _():
                c_zin(q).start()

    def s4(q):
        @pl.when(is_mid)
        def _():
            c_zmid(q).wait_recv()
            gath[q, my_rows, :] = ((zs[q].astype(F32) + zmid[q].astype(F32)) * scale).astype(BF16)
            c_gx(q).start()

            @pl.when(has_outer)
            def _():
                c_gz(q).start()

    def s5(q):
        @pl.when(not_mid)
        def _():
            c_gz(q).wait_recv()
            c_gx(q).start()

            @pl.when(has_outer)
            def _():
                c_gz(q).start()

    def s6(q):
        c_gx(q).wait_recv()
        finish(q)

    low_i = low.astype(jnp.int32)
    z_rows = pl.ds(pl.multiple_of((1 - low_i) * quarter, quarter), quarter)
    peer_rows = pl.ds(pl.multiple_of(low_i * quarter, quarter), quarter)

    def c_fin(q):
        return remote(fs.at[q], fin.at[q], ssem.at[ZIN, q], rsem.at[ZIN, q], to_in)

    def c_frs(q):
        return remote(fs.at[q, peer_rows], zmid.at[q], ssem.at[ZMID, q], rsem.at[ZMID, q], to_in)

    def c_fag(q):
        return remote(gath.at[q, z_rows], gath.at[q, z_rows], ssem.at[GX, q], rsem.at[GX, q], to_in)

    def c_fout(q):
        return remote(gath.at[q], gath.at[q], ssem.at[GZ, q], rsem.at[GZ, q], to_out)

    def f1(q):
        c_pair(q).wait_recv()

        @pl.when(jnp.logical_not(has_outer))
        def _():
            fs[q] = (own[q] + precv[q].astype(F32)).astype(BF16)

            @pl.when(is_mid)
            def _():
                c_frs(q).start()

            @pl.when(not_mid)
            def _():
                c_fin(q).start()

    def f2(q):
        @pl.when(has_outer)
        def _():
            c_fin(q).wait_recv()
            fs[q] = (own[q] + precv[q].astype(F32) + fin[q].astype(F32)).astype(BF16)

            @pl.when(is_mid)
            def _():
                c_frs(q).start()

            @pl.when(not_mid)
            def _():
                c_fin(q).start()

    def f3(q):
        @pl.when(is_mid)
        def _():
            c_frs(q).wait_recv()
            xsend[q] = (fs[q, z_rows, :].astype(F32) + zmid[q].astype(F32)).astype(BF16)
            c_xrs(q).start()

    def f4(q):
        @pl.when(is_mid)
        def _():
            c_xrs(q).wait_recv()
            gath[q, z_rows, :] = ((xsend[q].astype(F32) + xrecv[q].astype(F32)) * scale).astype(BF16)
            c_fag(q).start()

    def f5(q):
        @pl.when(is_mid)
        def _():
            c_fag(q).wait_recv()

            @pl.when(has_outer)
            def _():
                c_fout(q).start()

    def f6(q):
        @pl.when(not_mid)
        def _():
            c_fout(q).wait_recv()

            @pl.when(has_outer)
            def _():
                c_fout(q).start()

        finish(q)

    stages_a = [s1, lambda q: (s2(q), s2b(q)), s3, s4, s5, s6]
    stages_f = [f1, f2, f3, f4, f5, f6]
    offsets = [STEP * k for k in range(6)]
    route = [ROUTES[q % len(ROUTES)] for q in range(n_chunks)]

    def tick(t):
        for k in reversed(range(6)):
            q = t - offsets[k]
            if 0 <= q < n_chunks:
                (stages_a if route[q] == "A" else stages_f)[k](q)

    def conv(src, kernel_halves, m0, m):
        left = jnp.concatenate([src[m0 + a * cols : m0 + a * cols + m, :] for a in range(3)], axis=1)
        right = jnp.concatenate([kernel_halves[0], kernel_halves[1]], axis=1)
        return jnp.dot(left, right, preferred_element_type=F32)

    def conv_back(src, kernel_halves, m0, m):
        left, right = [], []
        for tap in range(9):
            a, b = tap // 3, tap % 3
            rows = slice(m0 + (2 - a) * cols, m0 + (2 - a) * cols + m)
            left.append(src[rows, (2 - b) * chans : (3 - b) * chans])
            right.append(kernel_halves[0, tap * chans : (tap + 1) * chans, :])
            right.append(kernel_halves[1, tap * chans : (tap + 1) * chans, :])
        return lax.dot_general(
            jnp.concatenate(left, axis=1),
            jnp.concatenate(right, axis=1),
            (((1,), (1,)), ((), ())),
            preferred_element_type=F32,
        )

    def terms(grad_t, src, which, a):
        field = src[a * cols : a * cols + cells, :]
        there = jnp.dot(
            grad_t[pl.ds(pl.multiple_of(other * half, half), half), :], field, preferred_element_type=F32
        ).astype(BF16)
        for s in range(sub):
            q = (which * 3 + a) * sub + s
            psend[q] = there[:, s * width : (s + 1) * width]
            c_pair(q).start()
        here = jnp.dot(
            grad_t[pl.ds(pl.multiple_of(me * half, half), half), :], field, preferred_element_type=F32
        )
        for s in range(sub):
            q = (which * 3 + a) * sub + s
            own[q] = here[:, s * width : (s + 1) * width]

    tile = min(256, cells)
    locals_[0].wait()
    spread(sx, xv[...].astype(F32), cols)
    locals_[2].wait()
    gt[...] = gv[...].astype(F32).T.astype(BF16)
    spread(sg, gv[...].astype(F32), cols)
    locals_[1].wait()
    wcopies[0].wait_recv()
    for m0 in range(0, cells, tile):
        pre[m0 : m0 + tile, :] = conv(sx, wb1, m0, tile)
    v = pre[...]
    hidden = (v / (1.0 + jnp.exp(-v))).astype(BF16)
    spread(sh, hidden.astype(F32), cols)
    for a in range(3):
        terms(gt, sh, 0, a)
    locals_[3].wait()
    wcopies[1].wait_recv()
    tick(0)
    for m0 in range(0, cells, tile):
        back = conv_back(sg, wb2, m0, tile)
        v = pre[m0 : m0 + tile, :]
        sigma = 1.0 / (1.0 + jnp.exp(-v))
        dpre = back * sigma * (1.0 + v * (1.0 - sigma))
        dt[:, m0 : m0 + tile] = dpre.T.astype(BF16)
    done = 1
    for t in range(1, sub):
        tick(t)
        done = t + 1
    for a in range(3):
        terms(dt, sx, 1, a)
        for _ in range(sub):
            tick(done)
            done += 1
    m_out = min(128, cells)
    for m0 in range(0, cells, m_out):
        total = conv(sh, wb2, m0, m_out) + xv[m0 : m0 + m_out, :].astype(F32)
        ov[m0 : m0 + m_out, :] = total.astype(BF16)
        if done < n_chunks + offsets[-1]:
            tick(done)
            done += 1
    out_copy = pltpu.make_async_copy(ov, out_hbm, lsem.at[4])
    out_copy.start()
    while done < n_chunks + offsets[-1]:
        tick(done)
        done += 1

    for copy in wcopies:
        copy.wait_send()
    for q in range(n_chunks):
        c_pair(q).wait_send()
        if route[q] == "A":
            c_xrs(q).wait_send()
            c_gx(q).wait_send()

            @pl.when(is_mid)
            def _():
                c_zmid(q).wait_send()

            @pl.when(not_mid)
            def _():
                c_zin(q).wait_send()

            @pl.when(has_outer)
            def _():
                c_gz(q).wait_send()

        else:

            @pl.when(is_mid)
            def _():
                c_frs(q).wait_send()
                c_xrs(q).wait_send()
                c_fag(q).wait_send()

            @pl.when(not_mid)
            def _():
                c_fin(q).wait_send()

            @pl.when(has_outer)
            def _():
                c_fout(q).wait_send()

        c_out(q).wait()
    out_copy.wait()


def body(mesh, inputs, cotangent, conv_first, conv_second):
    _, rows, cols, chans = inputs.shape
    cells = rows * cols
    half = chans // 2
    n = mesh.shape["dp"]
    scale = 1.0 / (inputs.shape[0] * n * mesh.shape["shard"])
    width = 3 * chans // SUB
    n_chunks = 6 * SUB
    hbm = pl.BlockSpec(memory_space=pl.ANY)
    vm = pltpu.VMEM
    outputs, second, first = pl.pallas_call(
        functools.partial(kernel, (n, cols, scale)),
        out_shape=(
            jax.ShapeDtypeStruct((cells, chans), BF16),
            jax.ShapeDtypeStruct((9, chans, half), BF16),
            jax.ShapeDtypeStruct((9, chans, half), BF16),
        ),
        in_specs=[hbm] * 4,
        out_specs=(hbm, hbm, hbm),
        scratch_shapes=[
            vm((cells, chans), BF16),
            vm((cells, chans), BF16),
            vm((2, 9 * chans, half), BF16),
            vm((2, 9 * chans, half), BF16),
            vm((cells + 2 * cols, 3 * chans), BF16),
            vm((cells + 2 * cols, 3 * chans), BF16),
            vm((cells + 2 * cols, 3 * chans), BF16),
            vm((cells, chans), F32),
            vm((chans, cells), BF16),
            vm((chans, cells), BF16),
            vm((cells, chans), BF16),
            vm((n_chunks, half, width), F32),
            vm((n_chunks, half, width), BF16),
            vm((n_chunks, half, width), BF16),
            vm((n_chunks, half // 2, width), BF16),
            vm((n_chunks, half // 2, width), BF16),
            vm((n_chunks, half // 2, width), BF16),
            vm((n_chunks, half // 2, width), BF16),
            vm((n_chunks, half // 2, width), BF16),
            vm((n_chunks, half, width), BF16),
            vm((n_chunks, half, width), BF16),
            vm((n_chunks, half, width), BF16),
            vm((n_chunks, width // chans, chans, half), BF16),
            pltpu.SemaphoreType.DMA((5,)),
            pltpu.SemaphoreType.DMA((2,)),
            pltpu.SemaphoreType.DMA((2,)),
            pltpu.SemaphoreType.DMA((6, n_chunks)),
            pltpu.SemaphoreType.DMA((6, n_chunks)),
            pltpu.SemaphoreType.DMA((n_chunks,)),
        ],
        compiler_params=pltpu.CompilerParams(
            collective_id=0, has_side_effects=True, vmem_limit_bytes=40 * 1024 * 1024
        ),
    )(
        pltpu.with_memory_space_constraint(inputs.reshape(cells, chans), pltpu.HBM),
        pltpu.with_memory_space_constraint(cotangent.reshape(cells, chans), pltpu.HBM),
        pltpu.with_memory_space_constraint(conv_first.reshape(9 * chans, half), pltpu.HBM),
        pltpu.with_memory_space_constraint(conv_second.reshape(9 * chans, half), pltpu.HBM),
    )

    return outputs.reshape(inputs.shape), first, second


def solution(mesh):
    placed = (
        P(("group", "dp", "shard"), None, None, None),
        P(("group", "dp", "shard"), None, None, None),
        P("group", None, "shard"),
        P("group", None, "shard"),
    )
    return jax.shard_map(
        functools.partial(body, mesh),
        mesh=mesh,
        in_specs=placed,
        out_specs=(
            P(("group", "dp", "shard"), None, None, None),
            P("group", None, "shard"),
            P("group", None, "shard"),
        ),
        check_vma=False,
    )
```

```python
import functools

import jax
import jax.numpy as jnp
from jax import lax
from jax.experimental import pallas as pl
from jax.experimental.pallas import tpu as pltpu
from jax.sharding import PartitionSpec as P

MESH = pl.DeviceIdType.MESH
F32 = jnp.float32
BF16 = jnp.bfloat16
SUB = 3
ROUTES = "A"
STEP = 6

PAIR, XRS, ZIN, ZMID, GZ, GX = range(6)


def remote(src, dst, ssem, rsem, dev):
    return pltpu.make_async_remote_copy(
        src_ref=src, dst_ref=dst, send_sem=ssem, recv_sem=rsem, device_id=dev, device_id_type=MESH
    )


def spread(dst, value, cols):
    cells, chans = value.shape
    j = lax.broadcasted_iota(jnp.int32, value.shape, 0) % cols
    zeros = jnp.zeros((cols, 3 * chans), BF16)
    dst[0:cols, :] = zeros
    dst[cells + cols : cells + 2 * cols, :] = zeros
    after = jnp.where(j == 0, 0.0, pltpu.roll(value, 1, 0))
    dst[cols : cells + cols, 0:chans] = after.astype(BF16)
    dst[cols : cells + cols, chans : 2 * chans] = value.astype(BF16)
    before = jnp.where(j == cols - 1, 0.0, pltpu.roll(value, cells - 1, 0))
    dst[cols : cells + cols, 2 * chans : 3 * chans] = before.astype(BF16)


def kernel(
    dims, x_hbm, g_hbm, w1_hbm, w2_hbm, out_ref, g2_ref, g1_ref,
    xv, gv, wb1, wb2, sx, sh, sg, pre, gt, dt,
    own, psend, precv, xsend, xrecv, zs, zin, zmid, gath, fs, fin,
    lsem, wsend, wrecv, ssem, rsem,
):
    n, cols, scale = dims
    cells, chans = xv.shape
    half = chans // 2
    quarter = half // 2
    n_chunks, _, width = own.shape
    sub = 3 * chans // width
    line = n // 2

    dp = lax.axis_index("dp")
    me = lax.axis_index("shard")
    other = 1 - me
    xi = dp % 2
    z = dp // 2
    low = z < line // 2
    inward = jnp.where(low, z + 1, z - 1)
    outward = jnp.where(low, z - 1, z + 1)
    has_outer = jnp.logical_and(z > 0, z < line - 1)
    is_mid = jnp.logical_or(z == line // 2 - 1, z == line // 2)
    not_mid = jnp.logical_not(is_mid)
    to_pair = {"shard": other}
    to_x = {"dp": z * 2 + 1 - xi}
    to_in = {"dp": inward * 2 + xi}
    to_out = {"dp": outward * 2 + xi}

    locals_ = [
        pltpu.make_async_copy(x_hbm, xv, lsem.at[0]),
        pltpu.make_async_copy(w1_hbm, wb1.at[me], lsem.at[1]),
        pltpu.make_async_copy(g_hbm, gv, lsem.at[2]),
        pltpu.make_async_copy(w2_hbm, wb2.at[me], lsem.at[3]),
    ]
    for copy in locals_:
        copy.start()

    barrier = pltpu.get_barrier_semaphore()
    for dev in (to_pair, to_x, to_in):
        pl.semaphore_signal(barrier, inc=1, device_id=dev, device_id_type=MESH)

    @pl.when(has_outer)
    def _():
        pl.semaphore_signal(barrier, inc=1, device_id=to_out, device_id_type=MESH)

    pl.semaphore_wait(barrier, 3 + has_outer.astype(jnp.int32))

    wcopies = [
        remote(w1_hbm, wb1.at[me], wsend.at[0], wrecv.at[0], to_pair),
        remote(w2_hbm, wb2.at[me], wsend.at[1], wrecv.at[1], to_pair),
    ]
    wcopies[0].start()

    my_rows = pl.ds(pl.multiple_of(xi * quarter, quarter), quarter)
    their_rows = pl.ds(pl.multiple_of((1 - xi) * quarter, quarter), quarter)

    def c_pair(q):
        return remote(psend.at[q], precv.at[q], ssem.at[PAIR, q], rsem.at[PAIR, q], to_pair)

    def c_xrs(q):
        return remote(xsend.at[q], xrecv.at[q], ssem.at[XRS, q], rsem.at[XRS, q], to_x)

    def c_zin(q):
        return remote(zs.at[q], zin.at[q], ssem.at[ZIN, q], rsem.at[ZIN, q], to_in)

    def c_zmid(q):
        return remote(zs.at[q], zmid.at[q], ssem.at[ZMID, q], rsem.at[ZMID, q], to_in)

    def c_gz(q):
        return remote(gath.at[q, my_rows], gath.at[q, my_rows], ssem.at[GZ, q], rsem.at[GZ, q], to_out)

    def c_gx(q):
        return remote(gath.at[q, my_rows], gath.at[q, my_rows], ssem.at[GX, q], rsem.at[GX, q], to_x)

    def finish(q):
        per = n_chunks // 2
        taps = width // chans
        dst = g2_ref if q < per else g1_ref
        for k in range(taps):
            dst[q % per * taps + k] = gath[q, :, k * chans : (k + 1) * chans].astype(F32).T.astype(BF16)

    def s1(q):
        c_pair(q).wait_recv()
        there = own[q, their_rows, :] + precv[q, their_rows, :].astype(F32)
        xsend[q] = there.astype(BF16)
        c_xrs(q).start()

    def s2(q):
        c_xrs(q).wait_recv()
        mine = own[q, my_rows, :] + precv[q, my_rows, :].astype(F32) + xrecv[q].astype(F32)

        @pl.when(has_outer)
        def _():
            own[q, my_rows, :] = mine

        @pl.when(jnp.logical_not(has_outer))
        def _():
            zs[q] = mine.astype(BF16)

    def s2b(q):
        @pl.when(jnp.logical_and(jnp.logical_not(has_outer), not_mid))
        def _():
            c_zin(q).start()

        @pl.when(jnp.logical_and(jnp.logical_not(has_outer), is_mid))
        def _():
            c_zmid(q).start()

    def s3(q):
        @pl.when(has_outer)
        def _():
            c_zin(q).wait_recv()
            zs[q] = (own[q, my_rows, :] + zin[q].astype(F32)).astype(BF16)

            @pl.when(is_mid)
            def _():
                c_zmid(q).start()

            @pl.when(not_mid)
            def _():
                c_zin(q).start()

    def s4(q):
        @pl.when(is_mid)
        def _():
            c_zmid(q).wait_recv()
            gath[q, my_rows, :] = ((zs[q].astype(F32) + zmid[q].astype(F32)) * scale).astype(BF16)
            c_gx(q).start()

            @pl.when(has_outer)
            def _():
                c_gz(q).start()

    def s5(q):
        @pl.when(not_mid)
        def _():
            c_gz(q).wait_recv()
            c_gx(q).start()

            @pl.when(has_outer)
            def _():
                c_gz(q).start()

    def s6(q):
        c_gx(q).wait_recv()
        finish(q)

    low_i = low.astype(jnp.int32)
    z_rows = pl.ds(pl.multiple_of((1 - low_i) * quarter, quarter), quarter)
    peer_rows = pl.ds(pl.multiple_of(low_i * quarter, quarter), quarter)

    def c_fin(q):
        return remote(fs.at[q], fin.at[q], ssem.at[ZIN, q], rsem.at[ZIN, q], to_in)

    def c_frs(q):
        return remote(fs.at[q, peer_rows], zmid.at[q], ssem.at[ZMID, q], rsem.at[ZMID, q], to_in)

    def c_fag(q):
        return remote(gath.at[q, z_rows], gath.at[q, z_rows], ssem.at[GX, q], rsem.at[GX, q], to_in)

    def c_fout(q):
        return remote(gath.at[q], gath.at[q], ssem.at[GZ, q], rsem.at[GZ, q], to_out)

    def f1(q):
        c_pair(q).wait_recv()

        @pl.when(jnp.logical_not(has_outer))
        def _():
            fs[q] = (own[q] + precv[q].astype(F32)).astype(BF16)

            @pl.when(is_mid)
            def _():
                c_frs(q).start()

            @pl.when(not_mid)
            def _():
                c_fin(q).start()

    def f2(q):
        @pl.when(has_outer)
        def _():
            c_fin(q).wait_recv()
            fs[q] = (own[q] + precv[q].astype(F32) + fin[q].astype(F32)).astype(BF16)

            @pl.when(is_mid)
            def _():
                c_frs(q).start()

            @pl.when(not_mid)
            def _():
                c_fin(q).start()

    def f3(q):
        @pl.when(is_mid)
        def _():
            c_frs(q).wait_recv()
            xsend[q] = (fs[q, z_rows, :].astype(F32) + zmid[q].astype(F32)).astype(BF16)
            c_xrs(q).start()

    def f4(q):
        @pl.when(is_mid)
        def _():
            c_xrs(q).wait_recv()
            gath[q, z_rows, :] = ((xsend[q].astype(F32) + xrecv[q].astype(F32)) * scale).astype(BF16)
            c_fag(q).start()

    def f5(q):
        @pl.when(is_mid)
        def _():
            c_fag(q).wait_recv()

            @pl.when(has_outer)
            def _():
                c_fout(q).start()

    def f6(q):
        @pl.when(not_mid)
        def _():
            c_fout(q).wait_recv()

            @pl.when(has_outer)
            def _():
                c_fout(q).start()

        finish(q)

    stages_a = [s1, lambda q: (s2(q), s2b(q)), s3, s4, s5, s6]
    stages_f = [f1, f2, f3, f4, f5, f6]
    offsets = [STEP * k for k in range(6)]
    route = [ROUTES[q % len(ROUTES)] for q in range(n_chunks)]

    def tick(t):
        for k in reversed(range(6)):
            q = t - offsets[k]
            if 0 <= q < n_chunks:
                (stages_a if route[q] == "A" else stages_f)[k](q)

    def conv(src, kernel_halves, m0, m):
        left = jnp.concatenate([src[m0 + a * cols : m0 + a * cols + m, :] for a in range(3)], axis=1)
        right = jnp.concatenate([kernel_halves[0], kernel_halves[1]], axis=1)
        return jnp.dot(left, right, preferred_element_type=F32)

    def conv_back(src, kernel_halves, m0, m):
        left, right = [], []
        for tap in range(9):
            a, b = tap // 3, tap % 3
            rows = slice(m0 + (2 - a) * cols, m0 + (2 - a) * cols + m)
            left.append(src[rows, (2 - b) * chans : (3 - b) * chans])
            right.append(kernel_halves[0, tap * chans : (tap + 1) * chans, :])
            right.append(kernel_halves[1, tap * chans : (tap + 1) * chans, :])
        return lax.dot_general(
            jnp.concatenate(left, axis=1),
            jnp.concatenate(right, axis=1),
            (((1,), (1,)), ((), ())),
            preferred_element_type=F32,
        )

    def terms(grad_t, src, which, a):
        field = src[a * cols : a * cols + cells, :]
        there = jnp.dot(
            grad_t[pl.ds(pl.multiple_of(other * half, half), half), :], field, preferred_element_type=F32
        ).astype(BF16)
        for s in range(sub):
            q = (which * 3 + a) * sub + s
            psend[q] = there[:, s * width : (s + 1) * width]
            c_pair(q).start()
        here = jnp.dot(
            grad_t[pl.ds(pl.multiple_of(me * half, half), half), :], field, preferred_element_type=F32
        )
        for s in range(sub):
            q = (which * 3 + a) * sub + s
            own[q] = here[:, s * width : (s + 1) * width]

    tile = min(256, cells)
    locals_[0].wait()
    spread(sx, xv[...].astype(F32), cols)
    locals_[2].wait()
    gt[...] = gv[...].astype(F32).T.astype(BF16)
    locals_[1].wait()
    wcopies[0].wait_recv()
    wcopies[1].start()
    for m0 in range(0, cells, tile):
        pre[m0 : m0 + tile, :] = conv(sx, wb1, m0, tile)
    v = pre[...]
    hidden = (v / (1.0 + jnp.exp(-v))).astype(BF16)
    spread(sh, hidden.astype(F32), cols)
    for a in range(3):
        terms(gt, sh, 0, a)
    spread(sg, gv[...].astype(F32), cols)
    locals_[3].wait()
    wcopies[1].wait_recv()
    tick(0)
    for m0 in range(0, cells, tile):
        back = conv_back(sg, wb2, m0, tile)
        v = pre[m0 : m0 + tile, :]
        sigma = 1.0 / (1.0 + jnp.exp(-v))
        dpre = back * sigma * (1.0 + v * (1.0 - sigma))
        dt[:, m0 : m0 + tile] = dpre.T.astype(BF16)
    done = 1
    for t in range(1, sub):
        tick(t)
        done = t + 1
    for a in range(3):
        terms(dt, sx, 1, a)
        for _ in range(sub):
            tick(done)
            done += 1
    m_out = min(128, cells)
    for m0 in range(0, cells, m_out):
        total = conv(sh, wb2, m0, m_out) + xv[m0 : m0 + m_out, :].astype(F32)
        out_ref[m0 : m0 + m_out, :] = total.astype(BF16)
        if done < n_chunks + offsets[-1]:
            tick(done)
            done += 1
    while done < n_chunks + offsets[-1]:
        tick(done)
        done += 1

    for copy in wcopies:
        copy.wait_send()
    for q in range(n_chunks):
        c_pair(q).wait_send()
        if route[q] == "A":
            c_xrs(q).wait_send()
            c_gx(q).wait_send()

            @pl.when(is_mid)
            def _():
                c_zmid(q).wait_send()

            @pl.when(not_mid)
            def _():
                c_zin(q).wait_send()

            @pl.when(has_outer)
            def _():
                c_gz(q).wait_send()

        else:

            @pl.when(is_mid)
            def _():
                c_frs(q).wait_send()
                c_xrs(q).wait_send()
                c_fag(q).wait_send()

            @pl.when(not_mid)
            def _():
                c_fin(q).wait_send()

            @pl.when(has_outer)
            def _():
                c_fout(q).wait_send()


def body(mesh, inputs, cotangent, conv_first, conv_second):
    _, rows, cols, chans = inputs.shape
    cells = rows * cols
    half = chans // 2
    n = mesh.shape["dp"]
    scale = 1.0 / (inputs.shape[0] * n * mesh.shape["shard"])
    width = 3 * chans // SUB
    n_chunks = 6 * SUB
    hbm = pl.BlockSpec(memory_space=pl.ANY)
    vm = pltpu.VMEM
    outputs, second, first = pl.pallas_call(
        functools.partial(kernel, (n, cols, scale)),
        out_shape=(
            jax.ShapeDtypeStruct((cells, chans), BF16),
            jax.ShapeDtypeStruct((9, chans, half), BF16),
            jax.ShapeDtypeStruct((9, chans, half), BF16),
        ),
        in_specs=[hbm] * 4,
        out_specs=(pl.BlockSpec(memory_space=vm),) * 3,
        scratch_shapes=[
            vm((cells, chans), BF16),
            vm((cells, chans), BF16),
            vm((2, 9 * chans, half), BF16),
            vm((2, 9 * chans, half), BF16),
            vm((cells + 2 * cols, 3 * chans), BF16),
            vm((cells + 2 * cols, 3 * chans), BF16),
            vm((cells + 2 * cols, 3 * chans), BF16),
            vm((cells, chans), F32),
            vm((chans, cells), BF16),
            vm((chans, cells), BF16),
            vm((n_chunks, half, width), F32),
            vm((n_chunks, half, width), BF16),
            vm((n_chunks, half, width), BF16),
            vm((n_chunks, half // 2, width), BF16),
            vm((n_chunks, half // 2, width), BF16),
            vm((n_chunks, half // 2, width), BF16),
            vm((n_chunks, half // 2, width), BF16),
            vm((n_chunks, half // 2, width), BF16),
            vm((n_chunks, half, width), BF16),
            vm((n_chunks, half, width), BF16),
            vm((n_chunks, half, width), BF16),
            pltpu.SemaphoreType.DMA((4,)),
            pltpu.SemaphoreType.DMA((2,)),
            pltpu.SemaphoreType.DMA((2,)),
            pltpu.SemaphoreType.DMA((6, n_chunks)),
            pltpu.SemaphoreType.DMA((6, n_chunks)),
        ],
        compiler_params=pltpu.CompilerParams(
            collective_id=0, has_side_effects=True, vmem_limit_bytes=40 * 1024 * 1024
        ),
    )(
        pltpu.with_memory_space_constraint(inputs.reshape(cells, chans), pltpu.HBM),
        pltpu.with_memory_space_constraint(cotangent.reshape(cells, chans), pltpu.HBM),
        pltpu.with_memory_space_constraint(conv_first.reshape(9 * chans, half), pltpu.HBM),
        pltpu.with_memory_space_constraint(conv_second.reshape(9 * chans, half), pltpu.HBM),
    )

    return outputs.reshape(inputs.shape), first, second


def solution(mesh):
    placed = (
        P(("group", "dp", "shard"), None, None, None),
        P(("group", "dp", "shard"), None, None, None),
        P("group", None, "shard"),
        P("group", None, "shard"),
    )
    return jax.shard_map(
        functools.partial(body, mesh),
        mesh=mesh,
        in_specs=placed,
        out_specs=(
            P(("group", "dp", "shard"), None, None, None),
            P("group", None, "shard"),
            P("group", None, "shard"),
        ),
        check_vma=False,
    )
```
